32 devices in a mesh: rep: 4 (over z), shard: 8 (over y, x, core).
Axes of the slice: x: 2, y: 2, z: 4, core: 2. Of those that a mesh axis runs over, the one named last changes fastest.
Arguments:
- tokens: bfloat16 [32, 256, 2048], P(('rep', 'shard')), may hold values from -6 to 6
- lengths: int32 [32], replicated, may hold values from 1 to 256, 6144 in all
- order: int32 [32], replicated, may hold values from 0 to 31, as said below
- norm_gain: bfloat16 [2, 2048], P(None, 'shard'), may hold values from 0.099609375 to 1.8984375
- in_proj: bfloat16 [2, 2048, 8512], P(None, 'shard'), may hold values from -0.125 to 0.125
- conv_weight: bfloat16 [2, 4, 4352], P(None, None, 'shard'), may hold values from -3 to 3
- conv_bias: bfloat16 [2, 4352], P(None, 'shard'), may hold values from -0.5 to 0.5
- dt_bias: bfloat16 [2, 64], P(None, 'shard'), may hold values from -6 to -2
- a_log: bfloat16 [2, 64], P(None, 'shard'), may hold values from 0 to 2.765625
- skip: bfloat16 [2, 64], P(None, 'shard'), may hold values from 0.5 to 1.5
- gate_norm: bfloat16 [2, 4096], P(None, 'shard'), may hold values from 0.099609375 to 1.8984375
- out_proj: bfloat16 [2, 4096, 2048], P(None, 'shard'), may hold values from -0.09375 to 0.09375
- cotangent: bfloat16 [32, 256, 2048], P(('rep', 'shard')), may hold values from -6 to 6
Outputs:
- output: bfloat16 [32, 256, 2048], P(('rep', 'shard'))
- grad_tokens: bfloat16 [32, 256, 2048], P(('rep', 'shard'))
- grad_norm_gain: float32 [2, 2048], P(None, 'shard')
- grad_in_proj: float32 [2, 2048, 8512], P(None, 'shard')
- grad_conv_weight: float32 [2, 4, 4352], P(None, None, 'shard')
- grad_conv_bias: float32 [2, 4352], P(None, 'shard')
- grad_dt_bias: float32 [2, 64], P(None, 'shard')
- grad_a_log: float32 [2, 64], P(None, 'shard')
- grad_skip: float32 [2, 64], P(None, 'shard')
- grad_gate_norm: float32 [2, 4096], P(None, 'shard')
- grad_out_proj: float32 [2, 4096, 2048], P(None, 'shard')
The draws below stay inside these ranges and needn't reach their ends.
Inputs may be any that keep to these rules, and one draw needn't show every extreme that they name: `lengths`: each length counts the valid leading positions of its sequence; one sequence fills all 256 positions in every draw. order is a permutation of the 32 sequences that maps each aligned block of 8 slots starting at a multiple of 8 onto the sequences with the same indices as a set.
All inputs are finite; a program needn't handle non-finite values.
Results may differ from the reference program's by a relative error of at most 0.02.
Values may be sent and summed in bfloat16 or wider, within the bound.
A program may use at most 768 MiB of HBM per device.

```python
import math
import jax
import jax.numpy as jnp
import numpy as np
from jax import lax

D = 2048
HEADS = 64
CONV = 4
SPAN = 256
LAYERS = 2
INNER = 4096
CONVCH = 4352
PROJ = 8512
CAP = 256
NSEQ = 32
GROUP_SEQS = 8


def group_permutation(single_key):
    return jax.random.permutation(single_key, GROUP_SEQS)


def draw_order(key, part):
    key = jax.random.fold_in(key, 7)
    groups = NSEQ // GROUP_SEQS
    group_keys = jax.random.split(key, groups)
    shuffled = jax.vmap(group_permutation)(group_keys).astype(jnp.int32)
    offsets = (jnp.arange(groups) * GROUP_SEQS).astype(jnp.int32)[:, None]
    return (shuffled + offsets).reshape(NSEQ).astype(jnp.int32)


def steps_of(rng, dims, pieces, smallest, largest):
    loudness, own = 1.0, jax.random.fold_in(rng, 6)
    for axis_at, shards_of in pieces:
        steps = jnp.exp(jax.random.uniform(jax.random.fold_in(own, axis_at), (shards_of,), jnp.float32, smallest / len(pieces), largest / len(pieces)))
        loudness = loudness * jnp.repeat(steps, dims[axis_at] // shards_of).reshape([-1 if axis == axis_at else 1 for axis in range(len(dims))])
    return loudness


def profile(number_of, total, most, skew):
    loads = [(1 << 20) // math.isqrt(standing ** skew) + 1 for standing in range(2, number_of + 1)]
    spare, holding = total - most - (number_of - 1), [1] * (number_of - 1)
    while spare > 0:
        candidates = [i for i in range(number_of - 1) if holding[i] < most]
        mass, left = sum([loads[i] for i in candidates]), spare
        for i in candidates:
            more = min(most - holding[i], max(1, left * loads[i] // mass), spare)
            holding[i] = holding[i] + more
            spare = spare - more
    return np.array([most] + holding)


def uneven(stream_key, amount, total, reach, skew):
    if amount == 2:
        one = jax.random.randint(stream_key, (), max(1, total - reach), min(reach, total - 1) + 1)
        return jnp.stack([one, total - one])
    sizes = jnp.asarray(profile(amount, total, reach, skew), jnp.int32)
    couples = (amount - 1) // 2
    giver, taker = sizes[1:1 + 2 * couples:2], sizes[2:2 + 2 * couples:2]
    margin = jnp.minimum(giver - 1, reach - taker)
    moved = jax.random.randint(jax.random.fold_in(stream_key, 1), (couples,), 0, 1 << 20) % (margin + 1)
    sizes = sizes.at[1:1 + 2 * couples:2].set(giver - moved).at[2:2 + 2 * couples:2].set(taker + moved)
    return sizes[jax.random.permutation(jax.random.fold_in(stream_key, 2), amount)]


def gaussian(key, shape, scale, limit, cuts=(), dtype=jnp.bfloat16):
    level = steps_of(key, shape, cuts, -0.22, 0.18) if cuts else 1.0
    entries = jax.random.normal(key, shape, jnp.float32) * scale * level
    return jnp.minimum(jnp.maximum(entries, -limit), limit).astype(dtype)


def setup_inputs(seed: int = 0) -> dict:
    seeds = jax.random.split(jax.random.key(seed), 14)
    tokens = gaussian(seeds[0], (NSEQ, CAP, D), 1.0, 6.0, ((0, 32),))
    lengths = uneven(seeds[1], NSEQ, NSEQ * CAP * 3 // 4, CAP, 0).astype(jnp.int32)
    order = draw_order(jax.random.fold_in(seeds[13], 71), 0)
    norm_gain = jnp.clip(1.0 + 0.18 * jax.random.normal(seeds[3], (LAYERS, D), jnp.float32), 0.099609375, 1.8984375).astype(jnp.bfloat16)
    in_proj = gaussian(seeds[4], (LAYERS, D, PROJ), D ** -0.5, 0.125, ((1, 8),))
    conv_weight = gaussian(seeds[5], (LAYERS, CONV, CONVCH), CONV ** -0.5, 3.0, ((2, 8),))
    conv_bias = jnp.clip(jax.random.uniform(seeds[6], (LAYERS, CONVCH), jnp.float32, -0.5, 0.5) * steps_of(seeds[6], (LAYERS, CONVCH), ((1, 8),), -0.4, 0.0), -0.5, 0.5).astype(jnp.bfloat16)
    dt_bias = jnp.clip(-6.0 + 4.0 * jax.random.uniform(seeds[7], (LAYERS, HEADS), jnp.float32) ** steps_of(seeds[7], (LAYERS, HEADS), ((1, 8),), -0.2, 0.2), -6.0, -2.0).astype(jnp.bfloat16)
    a_log = jnp.clip(2.765625 * jax.random.uniform(seeds[8], (LAYERS, HEADS), jnp.float32) ** steps_of(seeds[8], (LAYERS, HEADS), ((1, 8),), -0.2, 0.2), 0.0, 2.765625).astype(jnp.bfloat16)
    skip = jnp.clip(0.5 + 1.0 * jax.random.uniform(seeds[9], (LAYERS, HEADS), jnp.float32) ** steps_of(seeds[9], (LAYERS, HEADS), ((1, 8),), -0.2, 0.2), 0.5, 1.5).astype(jnp.bfloat16)
    gate_norm = jnp.clip(1.0 + 0.18 * jax.random.normal(seeds[10], (LAYERS, INNER), jnp.float32), 0.099609375, 1.8984375).astype(jnp.bfloat16)
    out_proj = gaussian(seeds[11], (LAYERS, INNER, D), INNER ** -0.5, 0.09375, ((1, 8),))
    cotangent = gaussian(seeds[12], (NSEQ, CAP, D), 1.0, 6.0, ((0, 32),))
    return dict(tokens=tokens, lengths=lengths, order=order, norm_gain=norm_gain, in_proj=in_proj, conv_weight=conv_weight, conv_bias=conv_bias, dt_bias=dt_bias, a_log=a_log, skip=skip, gate_norm=gate_norm, out_proj=out_proj, cotangent=cotangent)


EPS = 1e-05
HIGH = lax.Precision.HIGHEST

@jax.custom_vjp
def low(v):
    return lax.optimization_barrier(v.astype(jnp.bfloat16)).astype(jnp.float32)

@jax.custom_vjp
def low_back(v):
    return v

def low_keep(v):
    return (low(v), None)

def low_pass(kept, grad):
    return (grad,)

def back_keep(v):
    return (v, None)

def back_low(kept, grad):
    return (low(grad),)
low.defvjp(low_keep, low_pass)
low_back.defvjp(back_keep, back_low)

def rms_scale(stream, gain):
    return stream * lax.rsqrt(lax.optimization_barrier(jnp.mean(stream * stream, axis=-1, keepdims=True)) + EPS) * gain

def block_step(state_in, block):
    inputs_b, keys_b, queries_b, delta_b, logdec_b = block
    cumul = jnp.cumsum(logdec_b, axis=0)
    count = cumul.shape[0]
    causal = (jnp.arange(count)[:, None] >= jnp.arange(count)[None, :])[:, :, None]
    spread = cumul[:, None, :] - cumul[None, :, :]
    decay = jnp.where(causal, jnp.exp(jnp.where(causal, spread, 0.0)), 0.0)
    scores = jnp.dot(queries_b, keys_b.T, precision=HIGH)
    weights = scores[:, :, None] * decay * delta_b[None, :, :]
    intra = jnp.einsum('tsh,shp->thp', weights, inputs_b, precision=HIGH)
    inter = jnp.einsum('tn,hpn->thp', queries_b, state_in, precision=HIGH) * jnp.exp(cumul)[:, :, None]
    tail = jnp.exp(cumul[-1][None, :] - cumul) * delta_b
    carried = jnp.exp(cumul[-1])[:, None, None] * state_in + jnp.einsum('sh,sn,shp->hpn', tail, keys_b, inputs_b, precision=HIGH)
    return (carried, intra + inter)

def scan_blocks(inputs, keys, queries, delta, logdec):
    rows, heads, headdim = inputs.shape
    state = keys.shape[1]
    blocks = rows // SPAN
    packed = (inputs.reshape(blocks, SPAN, heads, headdim), keys.reshape(blocks, SPAN, state), queries.reshape(blocks, SPAN, state), delta.reshape(blocks, SPAN, heads), logdec.reshape(blocks, SPAN, heads))
    start = jnp.zeros((heads, headdim, state), jnp.float32)
    final, outputs = lax.scan(jax.checkpoint(block_step), start, packed)
    return outputs.reshape(rows, heads, headdim)

def mixer(projected, conv_weight, conv_bias, dt_bias, a_log, skip, gate_norm):
    inner = gate_norm.shape[0]
    heads = dt_bias.shape[0]
    headdim = inner // heads
    channels = conv_bias.shape[0]
    state = (channels - inner) // 2
    taps = conv_weight.shape[0]
    rows = projected.shape[0]
    gate_part = projected[:, :inner]
    conv_in = projected[:, inner:inner + channels]
    step_raw = projected[:, inner + channels:]
    padded = jnp.pad(conv_in, ((taps - 1, 0), (0, 0)))
    convolved = conv_bias + padded[0:rows] * conv_weight[0]
    for offset in range(1, taps):
        convolved = convolved + padded[offset:offset + rows] * conv_weight[offset]
    active = jax.nn.silu(convolved)
    inputs = active[:, :inner].reshape(rows, heads, headdim)
    keys = active[:, inner:inner + state]
    queries = active[:, inner + state:]
    delta = jax.nn.softplus(step_raw + dt_bias)
    logdec = -jnp.exp(a_log) * delta
    mixed = scan_blocks(inputs, keys, queries, delta, logdec) + skip[None, :, None] * inputs
    gated = mixed.reshape(rows, inner) * jax.nn.silu(gate_part)
    return rms_scale(gated, gate_norm)

def reference(tokens, lengths, order, norm_gain, in_proj, conv_weight, conv_bias, dt_bias, a_log, skip, gate_norm, out_proj, cotangent):
    weights = tuple((item.astype(jnp.float32) for item in (norm_gain, in_proj, conv_weight, conv_bias, dt_bias, a_log, skip, gate_norm, out_proj)))
    positions = jnp.arange(CAP).astype(jnp.int32)
    slots = jnp.arange(NSEQ).astype(jnp.int32)
    order = order.astype(jnp.int32)
    slot_lengths = lengths.astype(jnp.int32)[order]
    inverse = lax.optimization_barrier(jnp.sum(jnp.where(order[:, None] == slots[None, :], slots[:, None], 0), axis=0)).astype(jnp.int32)

    def forward(stream_all, params):

        def one_sequence(item):
            stream, length = item
            mask = (positions < length).astype(jnp.float32)[:, None]
            for layer in range(LAYERS):
                layer_params = tuple((entry[layer] for entry in params))
                normed = low(rms_scale(stream, layer_params[0]))
                projected = low_back(jnp.dot(normed, layer_params[1], precision=HIGH))
                gnorm = low(mixer(projected, layer_params[2], layer_params[3], layer_params[4], layer_params[5], layer_params[6], layer_params[7]))
                branch = low_back(jnp.dot(gnorm, layer_params[8], precision=HIGH))
                stream = stream + mask * branch
            return stream
        return lax.map(jax.checkpoint(one_sequence), (stream_all, slot_lengths))
    result, pull_back = jax.vjp(forward, tokens.astype(jnp.float32), weights)
    slot_cotangent = cotangent.astype(jnp.float32)[order]
    grad_stream, grads = pull_back(slot_cotangent)
    output = result[inverse].astype(jnp.bfloat16)
    grad_tokens = grad_stream[inverse].astype(jnp.bfloat16)
    return (output, grad_tokens, grads[0], grads[1], grads[2], grads[3], grads[4], grads[5], grads[6], grads[7], grads[8])
```

```python
import functools

import jax
import jax.numpy as jnp
from jax import lax
from jax.experimental import pallas as pl
from jax.experimental.pallas import tpu as pltpu
from jax.sharding import PartitionSpec as P

LAYERS = 2
EPS = 1e-05
HALF = 128
HEADDIM = 64
GROUP = 256
HPG = GROUP // HEADDIM
STATE = 128
NBC = 3 * STATE
STEPS = 16
LOG2E = 1.4426950408889634
HIGH = lax.Precision.HIGHEST
BF = jnp.bfloat16
F32 = jnp.float32


def nn(a, b, precision=None):
    return lax.dot_general(a, b, (((1,), (0,)), ((), ())), precision=precision, preferred_element_type=F32)


def nt(a, b, precision=None):
    return lax.dot_general(a, b, (((1,), (1,)), ((), ())), precision=precision, preferred_element_type=F32)


def tn(a, b, precision=None):
    return lax.dot_general(a, b, (((0,), (0,)), ((), ())), precision=precision, preferred_element_type=F32)


def sigm(v):
    return 0.5 * jnp.tanh(0.5 * v) + 0.5


def step_parts(v):
    u = jnp.exp(-jnp.abs(v))
    series = u * (1.0 - u * (0.5 - u * (1.0 / 3.0 - u * 0.25)))
    delta = jnp.maximum(v, 0.0) + jnp.where(u < 0.01, series, jnp.log(1.0 + u))
    inv = 1.0 / (1.0 + u)
    sig = jnp.where(v >= 0.0, inv, u * inv)
    safe = jnp.maximum(delta, 1e-30)
    logd = jnp.where(v < -15.0, v, jnp.log(safe))
    rho = jnp.where(v < -15.0, 1.0, sig / safe)
    return delta, sig, logd, rho


def iotas():
    row = lax.broadcasted_iota(jnp.int32, (HALF, HALF), 0)
    col = lax.broadcasted_iota(jnp.int32, (HALF, HALF), 1)
    return row, col


def conv_of(ext, weights, bias):
    out = bias + weights[0:1] * ext[5 : 5 + HALF, :]
    for tap in range(1, 4):
        out = out + weights[tap : tap + 1] * ext[5 + tap : 5 + tap + HALF, :]
    return out


def where_am_i():
    rep = lax.axis_index("rep")
    me = lax.axis_index("shard")
    return rep, me, me // 2, lax.rem(me, 2)


def chip_peer(k):
    rep, _, chip, core = where_am_i()
    return (rep, 2 * jnp.bitwise_xor(chip, k) + core)


def core_peer():
    rep, me, _, _ = where_am_i()
    return (rep, jnp.bitwise_xor(me, 1))


def greet(devices):
    barrier = pltpu.get_barrier_semaphore()
    for device in devices:
        pl.semaphore_signal(barrier, inc=1, device_id=device, device_id_type=pl.DeviceIdType.MESH)
    pl.semaphore_wait(barrier, len(devices))


def push(src, dst, sems, i, device):
    return pltpu.make_async_remote_copy(
        src_ref=src,
        dst_ref=dst,
        send_sem=sems.at[0, i],
        recv_sem=sems.at[1, i],
        device_id=device,
        device_id_type=pl.DeviceIdType.MESH,
    )


def relative(k, side):
    _, _, chip, core = where_am_i()
    return 2 * jnp.bitwise_xor(chip, k) + jnp.bitwise_xor(core, side)


def decay_parts(raw, pbc, lower):
    v = raw + pbc[4:5, 2 * STATE :]
    delta, sig, logd, rho = step_parts(v)
    cum = nn(lower, (LOG2E * pbc[5:6, 2 * STATE :]) * delta, HIGH)
    return delta, sig, rho, cum, cum - LOG2E * logd


def lanes_of(columns, rows):
    lane = lax.broadcasted_iota(jnp.int32, (rows, 128), 1)
    out = jnp.zeros((rows, 128), F32)
    for i, column in enumerate(columns):
        high = column.astype(BF).astype(F32)
        out = jnp.where(lane == 2 * i, high, jnp.where(lane == 2 * i + 1, column - high, out))
    return out.astype(BF)


def load_steps(blocks, wbc, wbc_s, steps):
    count = wbc[0].shape[0]
    part = wbc[0].shape[2]
    wbc_s[2 * STATE + STEPS :, :] = jnp.zeros_like(wbc_s[2 * STATE + STEPS :, :])
    for k in range(count):
        cols = slice(k * part, (k + 1) * part)
        wbc_s[0:STATE, cols] = wbc[0][k]
        wbc_s[STATE : 2 * STATE, cols] = wbc[1][k]
        rows = wbc[2][k]
        if steps < STEPS:
            _, _, chip, _ = where_am_i()
            shift = STEPS - lax.rem(chip * steps, STEPS)
            rows = pltpu.roll(rows.astype(F32), shift, 0)
            live = lax.broadcasted_iota(jnp.int32, rows.shape, 0) < steps
            rows = jnp.where(live, rows, 0.0).astype(BF)
        wbc_s[2 * STATE : 2 * STATE + STEPS, cols] = rows


def load_main(wz, wx, wm_s):
    for k in range(wz.shape[0]):
        cols = slice(k * wz.shape[2], (k + 1) * wz.shape[2])
        wm_s[0:GROUP, cols] = wz[k]
        wm_s[GROUP : 2 * GROUP, cols] = wx[k]


def fwd_kernel(nseq, ng, second, ins, outs, scratch):
    x_refs, refs = ins[:nseq], ins[nseq:]
    wz, wx, wb0, wb1, wdt, wo, pm, pbc = refs[:8]
    if second:
        st_in, hist_m, hist_bc = refs[8:]
    parts, xall, projz, projx, projbc, mixed = outs[:6]
    if not second:
        st_out = outs[6]
    acc, ext, b_s, c_s, s_s, cum_s, rt_s, tail_s, q_s, sq_s, wm_s, wbc_s = scratch
    width = acc.shape[1]
    part = width // (2 * nseq)
    g = pl.program_id(0)
    row, col = iotas()
    tri = row >= col
    left = col < HEADDIM

    @pl.when(g == 0)
    def _():
        for side in range(2):
            for k in range(nseq):
                at = pl.multiple_of(relative(k, side) * part, part)
                to = (side * nseq + k) * part
                for i in range(nseq):
                    xall[i * HALF : (i + 1) * HALF, to : to + part] = x_refs[i][:, pl.ds(at, part)]
        acc[...] = jnp.zeros_like(acc)
        sq_s[...] = jnp.zeros_like(sq_s)
        load_steps(2 * nseq, (wb0, wb1, wdt), wbc_s, ng * HPG)
        projbc[...] = nt(xall[...], wbc_s[...]).reshape(nseq, HALF, NBC)
        lower = jnp.where(tri, 1.0, 0.0)

        def one(s, carry):
            here = projbc[s]
            if second:
                ext[0:8, :] = hist_bc[s, :, : 2 * STATE]
            else:
                ext[0:8, :] = jnp.zeros((8, GROUP), F32)
            ext[8 : 8 + HALF, :] = here[:, : 2 * STATE]
            pre = conv_of(ext, pbc[0:4, : 2 * STATE], pbc[4:5, : 2 * STATE])
            act = pre * sigm(pre)
            keys = act[:, :STATE].astype(BF)
            queries = act[:, STATE:].astype(BF)
            b_s[s] = keys
            c_s[s] = queries
            s_s[s] = nt(queries, keys)
            _, _, _, cum, less = decay_parts(here[:, 2 * STATE :], pbc, lower)
            lesst = less.T
            for gg in range(ng):
                rt_s[gg, s, 0:HPG, :] = lesst[HPG * gg : HPG * (gg + 1), :]
                cum_s[gg, s] = cum if gg == 0 else pltpu.roll(cum, STATE - HPG * gg, 1)
            if not second:
                tail = jnp.exp2(cum[HALF - 1 : HALF, :] - less)
                for gg in range(ng):
                    tail_s[gg, s] = tail if gg == 0 else pltpu.roll(tail, STATE - HPG * gg, 1)
            return carry

        lax.fori_loop(0, nseq, one, 0)

    load_main(wz, wx, wm_s)
    proj = nt(xall[...], wm_s[...])
    projz[...] = proj[:, :GROUP].reshape(nseq, HALF, GROUP)
    projx[...] = proj[:, GROUP:].reshape(nseq, HALF, GROUP)
    params = pm[0]

    def group(s, carry):
        z = projz[s]
        if second:
            ext[0:8, :] = hist_m[s]
        else:
            ext[0:8, :] = jnp.zeros((8, GROUP), F32)
        ext[8 : 8 + HALF, :] = projx[s]
        pre = conv_of(ext, params[0:4], params[4:5])
        xs = pre * sigm(pre)
        xb = xs.astype(BF)
        scores = s_s[s]
        cg = cum_s[g, s]
        rt = rt_s[g, s]
        ys = []
        for pair in range(HPG // 2):
            lanes = slice(pair * 128, (pair + 1) * 128)
            ws, cols = [], []
            for j in (2 * pair, 2 * pair + 1):
                cb = jnp.broadcast_to(cg[:, j : j + 1], (HALF, HALF))
                e = jnp.exp2(jnp.where(tri, cb - rt[j : j + 1, :], -1e30))
                ws.append((e * scores).astype(BF))
                cols.append(cb)
            both = nn(jnp.concatenate(ws, 0), xb[:, lanes])
            y = jnp.where(left, both[:HALF], both[HALF:])
            if second:
                inter = nt(c_s[s], st_in[s, lanes, :].astype(BF))
                y = y + inter * jnp.exp2(jnp.where(left, cols[0], cols[1]))
            else:
                tg = tail_s[g, s]
                tb = jnp.where(left, tg[:, 2 * pair : 2 * pair + 1], tg[:, 2 * pair + 1 : 2 * pair + 2])
                st_out[s, lanes, :] = tn((xs[:, lanes] * tb).astype(BF), b_s[s])
            ys.append(y)
        mix = jnp.concatenate(ys, 1) + params[5:6] * xs
        mixed[s] = mix
        gated = mix * (z * sigm(z))
        here = pl.ds(pl.multiple_of(s * HALF, HALF), HALF)
        q_s[here, :] = (gated * params[6:7]).astype(BF)
        square = gated * gated
        sq_s[here, :] += square[:, :128] + square[:, 128:]
        return carry

    lax.fori_loop(0, nseq, group, 0)
    acc[...] += nn(q_s[...], wo[...])

    @pl.when(g == ng - 1)
    def _():
        for k in range(nseq):
            rows = slice(k * HALF, (k + 1) * HALF)
            parts[k, :, :width] = acc[rows, :].astype(BF)
            parts[k, :, width:] = lanes_of([jnp.sum(sq_s[rows, :], axis=1, keepdims=True)], HALF)


def bwd_kernel(nseq, ng, second, ins, outs, scratch):
    g_refs, t_refs, refs = ins[:nseq], ins[nseq : 2 * nseq], ins[2 * nseq :]
    wz, wx, wb0, wb1, wdt, wo, pm, pbc, projz, projx, projbc, mixed = refs[:12]
    refs = refs[12:]
    if second:
        st_in, hist_m, hist_bc = refs[:3]
    else:
        dst_in, head_m, head_bc = refs[:3]
    parts, gall, gpz, gpx, gpbc, gnorm, sgm, sgbc = outs[:8]
    if second:
        dst_out, hout_m, hout_bc = outs[8:]
    acc, ext, dext, b_s, c_s, s_s, ds_s, db_s, dc_s, cum_s, rt_s, tail_s, dq_s, plus_s, minus_s, csum_s, wm_s, wbc_s, r_b, s_b = scratch
    width = acc.shape[1]
    part = width // (2 * nseq)
    g = pl.program_id(0)
    row, col = iotas()
    tri = row >= col
    left = col < HEADDIM
    lower = jnp.where(tri, 1.0, 0.0)

    def load_bc(s):
        if second:
            ext[0:8, :] = hist_bc[s, :, : 2 * STATE]
        else:
            ext[0:8, :] = jnp.zeros((8, GROUP), F32)
        ext[8 : 8 + HALF, :] = projbc[s, :, : 2 * STATE]
        return conv_of(ext, pbc[0:4, : 2 * STATE], pbc[4:5, : 2 * STATE])

    @pl.when(g == 0)
    def _():
        for k in range(nseq):
            rows = slice(k * HALF, (k + 1) * HALF)
            gall[rows, :] = g_refs[k][...]
            scal = t_refs[k][...].astype(F32)
            r_b[rows, :] = jnp.broadcast_to(scal[:, 0:1] + scal[:, 1:2], (HALF, HALF))
            s_b[rows, :] = jnp.broadcast_to(scal[:, 2:3] + scal[:, 3:4], (HALF, HALF))
        acc[...] = jnp.zeros_like(acc)
        ds_s[...] = jnp.zeros_like(ds_s)
        db_s[...] = jnp.zeros_like(db_s)
        dc_s[...] = jnp.zeros_like(dc_s)
        plus_s[...] = jnp.zeros_like(plus_s)
        minus_s[...] = jnp.zeros_like(minus_s)
        csum_s[...] = jnp.zeros_like(csum_s)
        load_steps(2 * nseq, (wb0, wb1, wdt), wbc_s, ng * HPG)

        def one(s, carry):
            pre = load_bc(s)
            act = pre * sigm(pre)
            keys = act[:, :STATE].astype(BF)
            queries = act[:, STATE:].astype(BF)
            b_s[s] = keys
            c_s[s] = queries
            s_s[s] = nt(queries, keys)
            _, _, _, cum, less = decay_parts(projbc[s, :, 2 * STATE :], pbc, lower)
            lesst = less.T
            for gg in range(ng):
                rt_s[gg, s, 0:HPG, :] = lesst[HPG * gg : HPG * (gg + 1), :]
                cum_s[gg, s] = cum if gg == 0 else pltpu.roll(cum, STATE - HPG * gg, 1)
            if not second:
                tail = jnp.exp2(cum[HALF - 1 : HALF, :] - less)
                for gg in range(ng):
                    tail_s[gg, s] = tail if gg == 0 else pltpu.roll(tail, STATE - HPG * gg, 1)
            return carry

        lax.fori_loop(0, nseq, one, 0)

    dq_s[...] = nt(gall[...], wo[...])
    params = pm[0]
    sgm[...] = jnp.zeros_like(sgm)

    def group(s, carry):
        here = pl.ds(pl.multiple_of(s * HALF, HALF), HALF)
        if second:
            ext[0:8, :] = hist_m[s]
        else:
            ext[0:8, :] = jnp.zeros((8, GROUP), F32)
        ext[8 : 8 + HALF, :] = projx[s]
        pre = conv_of(ext, params[0:4], params[4:5])
        psig = sigm(pre)
        xs = pre * psig
        xb = xs.astype(BF)
        z = projz[s]
        mix = mixed[s]
        sig = sigm(z)
        zs = z * sig
        gated = mix * zs
        rr = r_b[here, :]
        ss = s_b[here, :]
        rr = jnp.concatenate([rr, rr], 1)
        ss = jnp.concatenate([ss, ss], 1)
        dqr = dq_s[here, :] * rr
        gnorm[s] = (gated * rr * params[6:7]).astype(BF)
        sgm[0, 6:7, :] += jnp.sum(dqr * gated, axis=0, keepdims=True)
        dgated = dqr * params[6:7] - ss * gated
        gpz[s] = (dgated * mix * (sig + zs * (1.0 - sig))).astype(BF)
        dmix = dgated * zs
        sgm[0, 5:6, :] += jnp.sum(dmix * xs, axis=0, keepdims=True)
        scores = s_s[s]
        cg = cum_s[g, s]
        rt = rt_s[g, s]
        dmb = dmix.astype(BF)
        dscore = ds_s[s]
        plus = plus_s[s]
        minus = minus_s[s]
        csum = []
        dxs = []
        for pair in range(HPG // 2):
            lanes = slice(pair * 128, (pair + 1) * 128)
            dm = dmix[:, lanes]
            db = dmb[:, lanes]
            zero = jnp.zeros_like(db)
            stack = jnp.concatenate([jnp.where(left, db, zero), jnp.where(left, zero, db)], 0)
            dws = nt(stack, xb[:, lanes])
            cbs = [jnp.broadcast_to(cg[:, j : j + 1], (HALF, HALF)) for j in (2 * pair, 2 * pair + 1)]
            if second:
                edge = jnp.exp2(jnp.where(left, cbs[0], cbs[1]))
                state = st_in[s, lanes, :].astype(BF)
                dye = dm * edge
                dyeb = dye.astype(BF)
                inner = dye * nt(c_s[s], state)
                dc_s[s] += nn(dyeb, state)
                dst_out[s, lanes, :] = tn(dyeb, c_s[s])
            else:
                tg = tail_s[g, s]
                tb = jnp.where(left, tg[:, 2 * pair : 2 * pair + 1], tg[:, 2 * pair + 1 : 2 * pair + 2])
                xst = xs[:, lanes] * tb
                dstate = dst_in[s, lanes, :].astype(BF)
                bds = nt(b_s[s], dstate)
                db_s[s] += nn(xst.astype(BF), dstate)
                inner = xst * bds
            ws = []
            for i, j in enumerate((2 * pair, 2 * pair + 1)):
                e = jnp.exp2(jnp.where(tri, cbs[i] - rt[j : j + 1, :], -1e30))
                ws.append((e * scores).astype(BF))
                t = dws[i * HALF : (i + 1) * HALF] * e
                dscore = dscore + t
                m = t * scores
                csum.append(jnp.sum(m, axis=0, keepdims=True))
                mine = left if i == 0 else jnp.logical_not(left)
                extra = jnp.where(mine, inner, 0.0)
                lane = col == HPG * g + j
                if second:
                    total = jnp.sum(m + extra, axis=1, keepdims=True)
                    plus = jnp.where(lane, total, plus)
                else:
                    plus = jnp.where(lane, jnp.sum(m, axis=1, keepdims=True), plus)
                    minus = jnp.where(lane, jnp.sum(extra, axis=1, keepdims=True), minus)
            dx = params[5:6, lanes] * dm + tn(jnp.concatenate(ws, 0), stack)
            if not second:
                dx = dx + tb * bds
            dxs.append(dx)
        ds_s[s] = dscore
        plus_s[s] = plus
        minus_s[s] = minus
        for j in range(HPG):
            csum_s[g, s, j : j + 1, :] = csum[j]
        dpre = jnp.concatenate(dxs, 1) * (psig + xs * (1.0 - psig))
        sgm[0, 4:5, :] += jnp.sum(dpre, axis=0, keepdims=True)
        dext[0:HALF, :] = dpre
        if second:
            dext[HALF : HALF + 8, :] = jnp.zeros((8, GROUP), F32)
            hout_m[s] = dpre[0:8, :]
        else:
            dext[HALF : HALF + 8, :] = head_m[s]
        dcin = jnp.zeros((HALF, GROUP), F32)
        for tap in range(4):
            sgm[0, tap : tap + 1, :] += jnp.sum(dpre * ext[5 + tap : 5 + tap + HALF, :], axis=0, keepdims=True)
            dcin = dcin + params[tap : tap + 1] * dext[3 - tap : 3 - tap + HALF, :]
        gpx[s] = dcin.astype(BF)
        return carry

    lax.fori_loop(0, nseq, group, 0)
    gz = gpz[...].reshape(nseq * HALF, GROUP)
    gx = gpx[...].reshape(nseq * HALF, GROUP)
    load_main(wz, wx, wm_s)
    acc[...] += nn(jnp.concatenate([gz, gx], 1), wm_s[...])

    @pl.when(g == ng - 1)
    def _():
        sgbc[...] = jnp.zeros_like(sgbc)
        upper = jnp.where(row <= col, 1.0, 0.0)

        def one(s, carry):
            pre = load_bc(s)
            psig = sigm(pre)
            act = pre * psig
            dsb = ds_s[s].astype(BF)
            dkeys = db_s[s] + tn(dsb, c_s[s])
            dqueries = dc_s[s] + nn(dsb, b_s[s])
            dpre = jnp.concatenate([dkeys, dqueries], 1) * (psig + act * (1.0 - psig))
            sgbc[4:5, : 2 * STATE] += jnp.sum(dpre, axis=0, keepdims=True)
            dext[0:HALF, :] = dpre
            if second:
                dext[HALF : HALF + 8, :] = jnp.zeros((8, GROUP), F32)
                hout_bc[s] = dpre[0:8, :]
            else:
                dext[HALF : HALF + 8, :] = head_bc[s]
            dcin = jnp.zeros((HALF, GROUP), F32)
            for tap in range(4):
                sgbc[tap : tap + 1, : 2 * STATE] += jnp.sum(
                    dpre * ext[5 + tap : 5 + tap + HALF, :], axis=0, keepdims=True
                )
                dcin = dcin + pbc[tap : tap + 1, : 2 * STATE] * dext[3 - tap : 3 - tap + HALF, :]
            gpbc[s, :, : 2 * STATE] = dcin.astype(BF)
            delta, sig, rho, _, _ = decay_parts(projbc[s, :, 2 * STATE :], pbc, lower)
            rate = pbc[5:6, 2 * STATE :]
            minus = minus_s[s]
            sums = [csum_s[gg, s, 0:HPG, :] for gg in range(ng)]
            sums = jnp.concatenate(sums + [jnp.zeros((STATE - ng * HPG, HALF), F32)], 0)
            direct = sums.T + minus
            last = jnp.where(row == HALF - 1, jnp.sum(minus, axis=0, keepdims=True), 0.0)
            dlog = nn(upper, plus_s[s] - direct + last, HIGH)
            sgbc[5:6, 2 * STATE :] += jnp.sum(dlog * rate * delta, axis=0, keepdims=True)
            dv = dlog * rate * sig + direct * rho
            sgbc[4:5, 2 * STATE :] += jnp.sum(dv, axis=0, keepdims=True)
            gpbc[s, :, 2 * STATE :] = dv.astype(BF)
            return carry

        lax.fori_loop(0, nseq, one, 0)
        gb = gpbc[...].reshape(nseq * HALF, NBC)
        acc[...] += nn(gb, wbc_s[...])
        for side in range(2):
            for k in range(nseq):
                to = pl.multiple_of(relative(k, side) * part, part)
                at = (side * nseq + k) * part
                for i in range(nseq):
                    parts[i, :, pl.ds(to, part)] = acc[i * HALF : (i + 1) * HALF, at : at + part].astype(BF)


ANY = pl.BlockSpec(memory_space=pl.ANY)


def whole(shape):
    return pl.BlockSpec(shape, lambda g: (0,) * len(shape))


def row_of(array, k, lanes=None, lane_block=0):
    lanes = array.shape[2] if lanes is None else lanes
    return (array, pl.BlockSpec((None, array.shape[1], lanes), lambda g: (k, 0, lane_block)))


def full(array):
    return (array, whole(array.shape))


def struct(shape, dtype):
    return jax.ShapeDtypeStruct(tuple(shape), dtype)


def vm(shape, dtype):
    return (struct(shape, dtype), whole(tuple(shape)))


def on_line(count):
    rep, me, _, _ = where_am_i()
    low = rep < count // 2
    depth = jnp.where(low, rep, count - 1 - rep)
    inner = jnp.where(low, rep + 1, rep - 1)
    outer = jnp.where(depth == 0, count - 1 - rep, jnp.where(low, rep - 1, rep + 1))
    return depth, (inner, me), (outer, me)


def peer_device(peer):
    rep, me, _, _ = where_am_i()
    if peer == "core":
        return core_peer()
    if peer == "pair":
        return (rep + 1 - 2 * lax.rem(rep, 2), me)
    if peer in ("inner", "outer"):
        _, inner, outer = on_line(lax.axis_size("rep"))
        return inner if peer == "inner" else outer
    return chip_peer(peer)


class Task:
    def __init__(self, ins, outs, scratch, start, finish, peers=()):
        self.ins, self.outs, self.scratch = ins, outs, scratch
        self.start, self.finish, self.peers = start, finish, peers


def launch(name, cid, steps, main, ins, outs, scratch, tasks, flops=0, limit=62):
    groups = [(ins, outs, scratch)] + [(task.ins, task.outs, task.scratch) for task in tasks]
    all_ins = sum((list(group[0]) for group in groups), [])
    all_outs = sum((list(group[1]) for group in groups), [])
    all_scratch = sum((list(group[2]) for group in groups), [])
    peers = []
    for task in tasks:
        for peer in task.peers:
            if peer not in peers:
                peers.append(peer)

    def split(refs, which):
        parts, at = [], 0
        for group in groups:
            count = len(group[which])
            parts.append(refs[at : at + count])
            at += count
        return parts

    def kernel(*refs):
        refs = list(refs)
        a, b = len(all_ins), len(all_ins) + len(all_outs)
        parts = list(zip(split(refs[:a], 0), split(refs[a:b], 1), split(refs[b:], 2)))
        g = pl.program_id(0)

        @pl.when(g == 0)
        def _():
            if peers:
                greet([peer_device(peer) for peer in peers])
            for task, part in zip(tasks, parts[1:]):
                task.start(*part)

        if main is not None:
            main(*parts[0])

        @pl.when(g == steps - 1)
        def _():
            for task, part in reversed(list(zip(tasks, parts[1:]))):
                task.finish(*part)

    params = dict(vmem_limit_bytes=limit << 20)
    if peers:
        params.update(collective_id=cid, has_side_effects=True)
    res = pl.pallas_call(
        kernel,
        grid=(steps,),
        in_specs=[spec for _, spec in all_ins],
        out_specs=[spec for _, spec in all_outs],
        out_shape=[shape for shape, _ in all_outs],
        scratch_shapes=all_scratch,
        compiler_params=pltpu.CompilerParams(**params),
        cost_estimate=pl.CostEstimate(flops=flops, bytes_accessed=40 << 20, transcendentals=0),
        name=name,
    )(*[array for array, _ in all_ins])
    return split(list(res), 1)


def gather_task(arrays, nch):
    count = len(arrays)

    def copies(ins, outs, scr):
        return [
            push(ins[i], outs[i].at[k - 1], scr[0], i * nch + k, chip_peer(k)) for k in range(1, nch) for i in range(count)
        ]

    def start(ins, outs, scr):
        for copy in copies(ins, outs, scr):
            copy.start()

    def finish(ins, outs, scr):
        for copy in copies(ins, outs, scr):
            copy.wait()

    return Task(
        [(array, ANY) for array in arrays],
        [(struct((nch - 1,) + array.shape, array.dtype), ANY) for array in arrays],
        [pltpu.SemaphoreType.DMA((2, count * nch))],
        start,
        finish,
        tuple(range(1, nch)),
    )


def collect_task(parts, ins, outs, scratch, work, share):
    nch = parts.shape[0]
    shared = []
    if share:
        last = outs[-1][0]
        shared = [(struct((nch - 1,) + last.shape, last.dtype), ANY)]

    def copies(ins, scr):
        return [push(ins[0].at[k], scr[1].at[k - 1], scr[0], k, chip_peer(k)) for k in range(1, nch)]

    def start(ins, outs, scr):
        for copy in copies(ins, scr):
            copy.start()

    def finish(ins, outs, scr):
        for copy in copies(ins, scr):
            copy.wait()

        def total(rows, cols):
            value = ins[1][rows, cols].astype(F32)
            for k in range(nch - 1):
                value = value + scr[1][k, rows, cols].astype(F32)
            return value

        work(total, ins[2:], outs, scr[2:])
        if share:
            sent = [push(outs[-2], outs[-1].at[k - 1], scr[0], nch + k, chip_peer(k)) for k in range(1, nch)]
            for copy in sent:
                copy.start()
            for copy in sent:
                copy.wait()

    return Task(
        [(parts, ANY), row_of(parts, 0)] + ins,
        outs + shared,
        [pltpu.SemaphoreType.DMA((2, 2 * nch)), pltpu.VMEM((nch - 1,) + parts.shape[1:], BF)] + scratch,
        start,
        finish,
        tuple(range(1, nch)),
    )


def by_rows(body):
    def step(i, carry):
        body(pl.ds(pl.multiple_of(i * 16, 16), 16))
        return carry

    lax.fori_loop(0, HALF // 16, step, 0)


def owner_fwd(parts, stream, mask, gain, gb, inner, share=False):
    width = stream[0].shape[-1]
    last = gain is None

    def work(total, ins, outs, scr):
        def body(rows):
            branch = total(rows, slice(0, width))
            tile = total(rows, slice(width, width + 128))
            scale = lax.rsqrt((tile[:, 0:1] + tile[:, 1:2]) * (1.0 / inner) + EPS)
            branch = branch * scale
            outs[0][rows, :] = branch
            value = ins[0][rows, :] + ins[1][rows, 0:1] * branch
            if last:
                outs[1][rows, :] = value.astype(BF)
                dots = jnp.sum(ins[2][rows, :].astype(F32) * branch, axis=1, keepdims=True)
                outs[2][rows, :] = lanes_of([scale, scale * scale * dots * (1.0 / inner)], 16)
            else:
                outs[1][rows, :] = value
                inv = lax.rsqrt(jnp.mean(value * value, axis=1, keepdims=True) + EPS)
                outs[2][rows, :] = (value * inv * ins[2][0:1, :]).astype(BF)
                outs[3][rows, :] = jnp.broadcast_to(scale, (16, 128))

        by_rows(body)

    shape = (HALF, width)
    outs = [vm(shape, F32), vm(shape, BF if last else F32)]
    outs += [vm((HALF, 128), BF)] if last else [vm(shape, BF), vm((HALF, 128), F32)]
    return collect_task(parts, [stream, full(mask), gb if last else gain], outs, [], work, share)


def owner_bwd(parts, stream, gain, flow, mask, branch, scale, inner):
    width = stream[0].shape[-1]
    first = branch is None

    def work(total, ins, outs, scr):
        outs[0][...] = jnp.zeros_like(outs[0])

        def body(rows):
            gx = total(rows, slice(0, width))
            value = ins[0][rows, :]
            inv = lax.rsqrt(jnp.mean(value * value, axis=1, keepdims=True) + EPS)
            outs[0][0:1, :] += jnp.sum(gx * value * inv, axis=0, keepdims=True)
            gs = gx * ins[1][0:1, :]
            coef = inv * inv * inv * jnp.mean(gs * value, axis=1, keepdims=True)
            new = ins[2][rows, :].astype(F32) + inv * gs - value * coef
            if first:
                outs[1][rows, :] = new.astype(BF)
            else:
                outs[1][rows, :] = new
                gb = (ins[3][rows, 0:1] * new).astype(BF)
                dots = jnp.sum(gb.astype(F32) * ins[4][rows, :], axis=1, keepdims=True)
                rate = ins[5][rows, 0:1]
                outs[2][rows, :width] = gb
                outs[2][rows, width:] = lanes_of([rate, rate * rate * dots * (1.0 / inner)], 16)

        by_rows(body)

    shape = (HALF, width)
    outs = [vm((8, width), F32), vm(shape, BF if first else F32)]
    ins = [stream, gain, flow]
    if not first:
        outs.append(vm((HALF, width + 128), BF))
        ins += [full(mask), full(branch), full(scale)]
    return collect_task(parts, ins, outs, [], work, False)


def group_out(nseq, inner, dtype):
    return (struct((nseq, HALF, inner), dtype), pl.BlockSpec((nseq, HALF, GROUP), lambda g: (0, 0, g)))


def weight_ins(w, wo, pm, pbc, layer):
    _, count, tall, part = w.shape
    width = wo.shape[1]
    at = (tall - STATE - STEPS) // STATE

    def rows(which, height, block):
        return (w, pl.BlockSpec((None, count, height, part), lambda g: (which, 0, block if block is not None else g, 0)))

    return [
        rows(0, GROUP, None),
        rows(1, GROUP, None),
        rows(0, STATE, at),
        rows(1, STATE, at),
        rows(0, STEPS, (tall - STEPS) // STEPS),
        (wo, pl.BlockSpec((GROUP, width), lambda g: (g, 0))),
        (pm, pl.BlockSpec((None, 1, 16, GROUP), lambda g: (layer, g, 0, 0))),
        (pbc, pl.BlockSpec((None, 8, NBC), lambda g: (layer, 0, 0))),
    ]


def grouped(array):
    count, rows, _ = array.shape
    return (array, pl.BlockSpec((count, rows, GROUP), lambda g: (0, 0, g)))


def grouped_tail(array):
    return (array, pl.BlockSpec((array.shape[0], 8, GROUP), lambda g: (0, HALF // 8 - 1, g)))


def state_of(array):
    return (array, pl.BlockSpec((array.shape[0], GROUP, STATE), lambda g: (0, g, 0)))


def bc_tail(array):
    return (array, pl.BlockSpec((array.shape[0], 8, NBC), lambda g: (0, HALF // 8 - 1, 0)))


def run_fwd(cid, xs, weights, previous, tasks):
    nseq = len(xs)
    wo = weights[5][0]
    inner, width = wo.shape
    ng = inner // GROUP
    rows = nseq * HALF
    second = previous is not None
    ins = list(xs) + list(weights)
    if second:
        ins += [state_of(previous["state"]), grouped_tail(previous["projx"]), bc_tail(previous["projbc"])]
    outs = [
        vm((nseq, HALF, width + 128), BF),
        vm((rows, width), BF),
        group_out(nseq, inner, F32),
        group_out(nseq, inner, F32),
        vm((nseq, HALF, NBC), F32),
        group_out(nseq, inner, F32),
    ]
    if not second:
        outs.append((struct((nseq, inner, STATE), F32), pl.BlockSpec((nseq, GROUP, STATE), lambda g: (0, g, 0))))
    scratch = [
        pltpu.VMEM((rows, width), F32),
        pltpu.VMEM((8 + HALF, GROUP), F32),
        pltpu.VMEM((nseq, HALF, STATE), BF),
        pltpu.VMEM((nseq, HALF, STATE), BF),
        pltpu.VMEM((nseq, HALF, HALF), F32),
        pltpu.VMEM((ng, nseq, HALF, STATE), F32),
        pltpu.VMEM((ng, nseq, 8, HALF), F32),
        pltpu.VMEM((ng, nseq, HALF, STATE), F32),
        pltpu.VMEM((rows, GROUP), BF),
        pltpu.VMEM((rows, 128), F32),
        pltpu.VMEM((2 * GROUP, width), BF),
        pltpu.VMEM((NBC, width), BF),
    ]
    name = "fwd_second" if second else "fwd_first"
    main = functools.partial(fwd_kernel, nseq, ng, second)
    res = launch(name, cid, ng, main, ins, outs, scratch, tasks, 4 * rows * width * (3 * inner + NBC))
    keys = ["parts", "xall", "projz", "projx", "projbc", "mixed", "state"]
    out = dict(zip(keys, res[0]))
    if second:
        out["state"] = previous["state"]
    return out, res[1:]


def run_bwd(cid, gs, scals, weights, saved, other, later, tasks):
    nseq = len(gs)
    wo = weights[5][0]
    inner, width = wo.shape
    ng = inner // GROUP
    rows = nseq * HALF
    second = later is None
    ins = list(gs) + list(scals) + list(weights)
    ins += [grouped(saved["projz"]), grouped(saved["projx"]), full(saved["projbc"]), grouped(saved["mixed"])]
    if second:
        ins += [state_of(other["state"]), grouped_tail(other["projx"]), bc_tail(other["projbc"])]
    else:
        ins += [state_of(later["dstate"]), grouped(later["head_m"]), full(later["head_bc"])]
    outs = [
        vm((nseq, HALF, width), BF),
        vm((rows, width), BF),
        group_out(nseq, inner, BF),
        group_out(nseq, inner, BF),
        vm((nseq, HALF, NBC), BF),
        group_out(nseq, inner, BF),
        (struct((ng, 8, GROUP), F32), pl.BlockSpec((1, 8, GROUP), lambda g: (g, 0, 0))),
        vm((8, NBC), F32),
    ]
    if second:
        outs += [
            (struct((nseq, inner, STATE), F32), pl.BlockSpec((nseq, GROUP, STATE), lambda g: (0, g, 0))),
            (struct((nseq, 8, inner), F32), pl.BlockSpec((nseq, 8, GROUP), lambda g: (0, 0, g))),
            vm((nseq, 8, GROUP), F32),
        ]
    square = pltpu.VMEM((nseq, HALF, HALF), F32)
    scratch = [
        pltpu.VMEM((rows, width), F32),
        pltpu.VMEM((8 + HALF, GROUP), F32),
        pltpu.VMEM((8 + HALF, GROUP), F32),
        pltpu.VMEM((nseq, HALF, STATE), BF),
        pltpu.VMEM((nseq, HALF, STATE), BF),
        square,
        square,
        square,
        square,
        pltpu.VMEM((ng, nseq, HALF, STATE), F32),
        pltpu.VMEM((ng, nseq, 8, HALF), F32),
        pltpu.VMEM((ng, nseq, HALF, STATE), F32),
        pltpu.VMEM((rows, GROUP), F32),
        square,
        square,
        pltpu.VMEM((ng, nseq, 8, HALF), F32),
        pltpu.VMEM((2 * GROUP, width), BF),
        pltpu.VMEM((NBC, width), BF),
        pltpu.VMEM((rows, HALF), F32),
        pltpu.VMEM((rows, HALF), F32),
    ]
    name = "bwd_second" if second else "bwd_first"
    main = functools.partial(bwd_kernel, nseq, ng, second)
    res = launch(name, cid, ng, main, ins, outs, scratch, tasks, 8 * rows * width * (3 * inner + NBC))
    keys = ["parts", "gall", "gpz", "gpx", "gpbc", "gnorm", "sgm", "sgbc", "dstate", "head_m", "head_bc"]
    return dict(zip(keys, res[0])), res[1:]


def grads_task(nch, xa, xb, za, zb, ma, mb, ba, bb, qa, qb, ga, gb):
    rows, width = xa.shape
    local = za.shape[1]
    part = width // (2 * nch)
    tall = 2 * local + 2 * STATE + STEPS
    half = local // 2

    quarter = half // 4
    block = 256

    def halves(ins, side, put_in, put_out, before, after):
        xa, xb, za, zb, ma, mb, ba, bb, qa, qb, ga, gb = ins
        _, _, _, core = where_am_i()
        for k in range(nch):
            before(k)
            cols = slice((side * nch + k) * part, (side * nch + k + 1) * part)
            ax, bx = xa[:, cols], xb[:, cols]
            for i, (a, b) in enumerate(((za, zb), (ma, mb))):
                for at in range(0, local, 512):
                    span = slice(at, at + 512)
                    put_in(k, i * local + at, tn(a[:, span], ax) + tn(b[:, span], bx))
            value = tn(ba[...], ax) + tn(bb[...], bx)
            put_in(k, 2 * local, value[: 2 * STATE + STEPS])
            after(k)
        before(nch)
        base = jnp.bitwise_xor(core, side) * half
        for at in range(0, half, block):
            span = pl.ds(pl.multiple_of(base + at, block), block)
            aq, bq = qa[:, span], qb[:, span]
            for lane in range(0, width, 512):
                cols = slice(lane, lane + 512)
                put_out(at, cols, tn(aq, ga[:, cols]) + tn(bq, gb[:, cols]))
        after(nch)

    def nothing(k):
        return None

    def copies(scr, k):
        sems, away_in, away_out, came_in, came_out = scr
        if k == nch:
            return push(away_out, came_out, sems, nch, core_peer())
        return push(away_in.at[k], came_in.at[k], sems, k, core_peer())

    def start(ins, outs, scr):
        _, away_in, away_out, _, _ = scr

        def put_in(k, at, value):
            away_in[k, at : at + value.shape[0], :] = value.astype(BF)

        def put_out(at, cols, value):
            away_out[at : at + block, cols] = value.astype(BF)

        halves(ins, 1, put_in, put_out, nothing, lambda k: copies(scr, k).start())

    def finish(ins, outs, scr):
        _, _, _, came_in, came_out = scr

        def put_in(k, at, value):
            rows = slice(at, at + value.shape[0])
            outs[k][rows, :] = (value + came_in[k, rows, :].astype(F32)).astype(BF)

        def put_out(at, cols, value):
            for row in range(at, at + block, min(quarter, block)):
                i, to = divmod(row, quarter)
                size = min(quarter, block)
                piece = value[row - at : row - at + size] + came_out[row : row + size, cols].astype(F32)
                outs[nch + i][to : to + size, cols] = piece.astype(BF)

        halves(ins, 0, put_in, put_out, lambda k: copies(scr, k).wait(), nothing)

    arrays = [xa, xb, za, zb, ma, mb, ba, bb, qa, qb, ga, gb]
    big, small = (nch, tall, part), (half, width)
    return Task(
        [full(array) for array in arrays],
        [vm((tall, part), BF)] * nch + [vm((quarter, width), BF)] * 4,
        [pltpu.SemaphoreType.DMA((2, nch + 1))]
        + [pltpu.VMEM(big, BF), pltpu.VMEM(small, BF), pltpu.VMEM(big, BF), pltpu.VMEM(small, BF)],
        start,
        finish,
        ("core",),
    )


def pieces_of(to, which, nch, inner, channels):
    local = inner // nch
    steps = local // HEADDIM
    first = pl.multiple_of(which * inner + to * local, GROUP)
    second = pl.multiple_of(2 * inner + which * STATE, STATE)
    third = pl.multiple_of(inner + channels + (to * steps) // STEPS * STEPS, STEPS)
    return [(first, 0, local), (second, local, STATE), (third, local + STATE, STEPS)]


def start_kernel(
    nch, inner, channels, tr, tokens, small, out_proj, w, toks, smalls, wo0, wo1, sems, local_sems, own_w, own_t, own_s, own_o
):
    rep, me, chip, core = where_am_i()
    zpar = lax.rem(rep, 2)
    zdev = (rep + 1 - 2 * zpar, me)
    cdev = core_peer()
    greet([chip_peer(k) for k in range(1, nch)] + [cdev, zdev])
    number = iter(range(1000))
    waits, loads, stores = [], [], []

    def go(src, dst, device):
        copy = push(src, dst, sems, next(number), device)
        copy.start()
        waits.append(copy)
        return copy

    def here(src, stage, dst):
        i = len(loads)
        load = pltpu.make_async_copy(src, stage, local_sems.at[0, i])
        load.start()
        loads.append(load)
        stores.append(pltpu.make_async_copy(stage, dst, local_sems.at[1, i]))

    def rows(ref, at, count):
        return ref.at[pl.ds(at, count), :]

    fetched = []
    for k in range(1, nch):
        to = jnp.bitwise_xor(chip, k)
        fetched.append(
            [
                go(rows(tr.at[0], at, count), rows(w.at[zpar, k], put, count), chip_peer(k))
                for at, put, count in pieces_of(to, zpar, nch, inner, channels)
            ]
        )
    got_small = [go(small, smalls.at[k], chip_peer(k)) for k in range(1, nch)]
    got_first = [go(rows(tokens.at[0], 0, HALF), toks.at[k, pl.ds(0, HALF), :], chip_peer(k)) for k in range(1, nch)]
    for which in range(2):
        for at, put, count in pieces_of(chip, which, nch, inner, channels):
            here(rows(tr.at[0], at, count), rows(own_w.at[which], put, count), rows(w.at[which, 0], put, count))
            go(rows(tr.at[0], at, count), rows(w.at[which, nch], put, count), cdev)
    here(small, own_s, smalls.at[0])
    here(tokens.at[0], own_t, toks.at[0])
    go(small, smalls.at[nch], cdev)
    go(tokens.at[0], toks.at[nch], cdev)
    half = out_proj.shape[1]
    at = pl.multiple_of(core * half, half)
    for layer, wo in enumerate((wo0, wo1)):
        here(out_proj.at[layer], own_o.at[layer], rows(wo, at, half))
        go(out_proj.at[layer], rows(wo, at, half), cdev)
    for load, store in zip(loads, stores):
        load.wait()
        store.start()
    swapped = []
    for k in range(1, nch):
        for copy in fetched[k - 1]:
            copy.wait_recv()
        swapped.append(go(w.at[zpar, k], w.at[zpar, k], zdev))
        go(w.at[zpar, k], w.at[zpar, nch + k], cdev)
    got_last = [
        go(rows(tokens.at[0], HALF, HALF), toks.at[k, pl.ds(HALF, HALF), :], chip_peer(k)) for k in range(1, nch)
    ]
    for k in range(1, nch):
        got_small[k - 1].wait_recv()
        go(smalls.at[k], smalls.at[nch + k], cdev)
        got_first[k - 1].wait_recv()
        go(toks.at[k, pl.ds(0, HALF), :], toks.at[nch + k, pl.ds(0, HALF), :], cdev)
    for k in range(1, nch):
        swapped[k - 1].wait_recv()
        go(w.at[1 - zpar, k], w.at[1 - zpar, nch + k], cdev)
    for k in range(1, nch):
        got_last[k - 1].wait_recv()
        go(toks.at[k, pl.ds(HALF, HALF), :], toks.at[nch + k, pl.ds(HALF, HALF), :], cdev)
    received = set(map(id, sum(fetched, []) + got_small + got_first + got_last + swapped))
    for copy in waits:
        copy.wait_send()
        if id(copy) not in received:
            copy.wait_recv()
    for copy in stores:
        copy.wait()


def start_up(tr, tokens, small, out_proj, nch, inner, channels):
    n = 2 * nch
    local = inner // nch
    part = tr.shape[2]
    width = tokens.shape[2]
    outs = [
        struct((2, n, local + STATE + STEPS, part), BF),
        struct((n,) + tokens.shape[1:], BF),
        struct((n,) + small.shape, BF),
        struct((local, width), BF),
        struct((local, width), BF),
    ]
    return pl.pallas_call(
        functools.partial(start_kernel, nch, inner, channels),
        in_specs=[ANY] * 4,
        out_specs=[ANY] * 5,
        out_shape=outs,
        scratch_shapes=[
            pltpu.SemaphoreType.DMA((2, 16 * nch + 16)),
            pltpu.SemaphoreType.DMA((2, 16)),
            pltpu.VMEM((2, local + STATE + STEPS, part), BF),
            pltpu.VMEM(tokens.shape[1:], BF),
            pltpu.VMEM(small.shape, BF),
            pltpu.VMEM(out_proj.shape, BF),
        ],
        compiler_params=pltpu.CompilerParams(collective_id=1, has_side_effects=True, vmem_limit_bytes=40 << 20),
        name="start_up",
    )(tr, tokens, small, out_proj)


def fetch_task(tr, layer, nch, inner, channels):
    tall = inner // nch + STATE + STEPS

    def copies(ins, outs, scr):
        rep, _, chip, _ = where_am_i()
        zpar = lax.rem(rep, 2)
        out = []
        for k in range(1, nch):
            to = jnp.bitwise_xor(chip, k)
            for i, (at, put, count) in enumerate(pieces_of(to, zpar, nch, inner, channels)):
                src = ins[0].at[layer, pl.ds(at, count), :]
                out.append(push(src, outs[0].at[k - 1, pl.ds(put, count), :], scr[0], 3 * k + i, chip_peer(k)))
        return out

    def start(ins, outs, scr):
        for copy in copies(ins, outs, scr):
            copy.start()

    def finish(ins, outs, scr):
        for copy in copies(ins, outs, scr):
            copy.wait()

    return Task(
        [(tr, ANY)],
        [(struct((nch - 1, tall, tr.shape[2]), BF), ANY)],
        [pltpu.SemaphoreType.DMA((2, 3 * nch))],
        start,
        finish,
        tuple(range(1, nch)),
    )


def finish_task(tr, fetched, layer, nch, inner, channels):
    n = 2 * nch
    tall = inner // nch + STATE + STEPS

    def plan(ins, outs, scr):
        rep, me, chip, core = where_am_i()
        zpar = lax.rem(rep, 2)
        zdev = (rep + 1 - 2 * zpar, me)
        cdev = core_peer()
        source, got, w = ins[0], ins[1], outs[0]
        near, far, here = [], [], []
        for k in range(1, nch):
            near.append(push(got.at[k - 1], w.at[zpar, k], scr[0], k, zdev))
            near.append(push(got.at[k - 1], w.at[zpar, nch + k], scr[0], nch + k, cdev))
            far.append(push(w.at[1 - zpar, k], w.at[1 - zpar, nch + k], scr[0], 2 * nch + k, cdev))
            here.append((got.at[k - 1], scr[2].at[k - 1], w.at[zpar, k]))
        i = 0
        for which in range(2):
            for at, put, count in pieces_of(chip, which, nch, inner, channels):
                src = source.at[layer, pl.ds(at, count), :]
                near.append(push(src, w.at[which, nch, pl.ds(put, count), :], scr[0], 3 * nch + i, cdev))
                stage = scr[2].at[nch - 1 + which, pl.ds(put, count), :]
                here.append((src, stage, w.at[which, 0, pl.ds(put, count), :]))
                i += 1
        loads = [pltpu.make_async_copy(src, stage, scr[1].at[0, i]) for i, (src, stage, _) in enumerate(here)]
        stores = [pltpu.make_async_copy(stage, dst, scr[1].at[1, i]) for i, (_, stage, dst) in enumerate(here)]
        return near, far, loads, stores

    def start(ins, outs, scr):
        near, _, loads, stores = plan(ins, outs, scr)
        for copy in near + loads:
            copy.start()
        for load, store in zip(loads, stores):
            load.wait()
            store.start()

    def finish(ins, outs, scr):
        near, far, _, stores = plan(ins, outs, scr)
        for k in range(1, nch):
            near[2 * (k - 1)].wait_recv()
            far[k - 1].start()
        for copy in stores:
            copy.wait()
        for i, copy in enumerate(near):
            copy.wait_send()
            if i >= 2 * (nch - 1) or i % 2:
                copy.wait_recv()
        for copy in far:
            copy.wait()

    return Task(
        [(tr, ANY), (fetched, ANY)],
        [(struct((2, n, tall, tr.shape[2]), BF), ANY)],
        [
            pltpu.SemaphoreType.DMA((2, 3 * nch + 6)),
            pltpu.SemaphoreType.DMA((2, nch + 6)),
            pltpu.VMEM((nch + 1, tall, tr.shape[2]), BF),
        ],
        start,
        finish,
        tuple(range(1, nch)) + ("core", "pair"),
    )


def params_kernel(nch, n, sizes, index, small, gains, pm, pbc, full_s):
    chip, core = index[0], index[1]
    part, gate_n, conv_n, head_n = sizes
    _, ng, _, _ = pm.shape
    local = ng * GROUP
    steps = 2 * head_n
    at_dt = part + gate_n
    row = lax.broadcasted_iota(jnp.int32, (STATE, local), 0)
    col = lax.broadcasted_iota(jnp.int32, (STATE, local), 1)
    expand = jnp.where(col // HEADDIM == row, 1.0, 0.0).astype(BF)
    lane = lax.broadcasted_iota(jnp.int32, (1, STATE), 1)

    def rel(q):
        return jnp.bitwise_xor(core, q % 2) * nch + jnp.bitwise_xor(chip, q // 2)

    for q in range(n):
        here = small[rel(q)].astype(F32)
        for layer in range(LAYERS):
            gains[layer, :, q * part : (q + 1) * part] = jnp.broadcast_to(here[8 * layer : 8 * layer + 1, :part], (8, part))
            full_s[8 * layer : 8 * layer + 5, q * conv_n : (q + 1) * conv_n] = here[8 * layer + 1 : 8 * layer + 6, :conv_n]
    own = [small[jnp.bitwise_xor(core, c) * nch].astype(F32) for c in range(2)]
    pm[...] = jnp.zeros_like(pm)
    pbc[...] = jnp.zeros_like(pbc)
    for layer in range(LAYERS):
        top = [item[8 * layer : 8 * layer + 1] for item in own]

        def heads(at):
            first = jnp.where(lane < head_n, top[0][:, at : at + STATE], 0.0)
            last = jnp.where(lane < head_n, top[1][:, at : at + STATE], 0.0)
            return first + pltpu.roll(last, head_n, 1)

        skip = nn(jnp.broadcast_to(heads(at_dt + 2 * STATE), (8, STATE)).astype(BF), expand)
        for g in range(ng):
            cols = pl.ds(pl.multiple_of(chip * local + g * GROUP, GROUP), GROUP)
            pm[layer, g, 0:5, :] = full_s[8 * layer : 8 * layer + 5, cols]
            pm[layer, g, 5:6, :] = skip[0:1, g * GROUP : (g + 1) * GROUP]
            which, at = divmod(g * GROUP, gate_n)
            pm[layer, g, 6:7, :] = top[which][:, part + at : part + at + GROUP]
        inner = nch * local
        pbc[layer, 0:5, : 2 * STATE] = full_s[8 * layer : 8 * layer + 5, inner : inner + 2 * STATE]
        pbc[layer, 4:5, 2 * STATE :] = heads(at_dt)
        pbc[layer, 5:6, 2 * STATE :] = jnp.where(lane < steps, -jnp.exp(heads(at_dt + STATE)), 0.0)


def make_params(index, small, nch, ng, sizes):
    n = 2 * nch
    width = small.shape[2]
    part, gate_n, conv_n, head_n = sizes
    shapes = [(LAYERS, 8, width), (LAYERS, ng, 16, GROUP), (LAYERS, 8, NBC)]
    return pl.pallas_call(
        functools.partial(params_kernel, nch, n, sizes),
        grid_spec=pltpu.PrefetchScalarGridSpec(
            num_scalar_prefetch=1,
            grid=(1,),
            in_specs=[pl.BlockSpec(small.shape, lambda i, idx: (0, 0, 0))],
            out_specs=[pl.BlockSpec(shape, lambda i, idx, m=len(shape): (0,) * m) for shape in shapes],
            scratch_shapes=[pltpu.VMEM((16, n * conv_n), F32)],
        ),
        out_shape=[struct(shape, F32) for shape in shapes],
        name="params",
    )(index, small)


def pick_kernel(slots, tok, gain, xs, stream):
    value = tok[...].astype(F32)
    inv = lax.rsqrt(jnp.mean(value * value, axis=1, keepdims=True) + EPS)
    xs[...] = (value * inv * gain[0:1, :]).astype(BF)

    @pl.when(pl.program_id(1) == 0)
    def _():
        stream[...] = value


def pick(slots, toks, gains, nch):
    _, rows, width = toks.shape
    return pl.pallas_call(
        pick_kernel,
        grid_spec=pltpu.PrefetchScalarGridSpec(
            num_scalar_prefetch=1,
            grid=(rows // HALF, nch),
            in_specs=[
                pl.BlockSpec((None, HALF, width), lambda h, k, idx: (idx[k], h, 0)),
                pl.BlockSpec((None, 8, width), lambda h, k, idx: (0, 0, 0)),
            ],
            out_specs=[
                pl.BlockSpec((None, None, HALF, width), lambda h, k, idx: (h, k, 0, 0)),
                pl.BlockSpec((None, HALF, width), lambda h, k, idx: (h, 0, 0)),
            ],
        ),
        out_shape=[struct((rows // HALF, nch, HALF, width), BF), struct((rows // HALF, HALF, width), F32)],
        name="pick",
    )(slots, toks, gains)


def hop_task(hop, arrays):
    count = lax.axis_size("rep")
    mid = count // 2
    total = len(arrays)
    inward, exchange = hop < mid - 1, hop == mid - 1
    sender = min(hop, 2 * mid - 1 - hop)
    taker = sender if exchange else sender + (1 if inward else -1)

    def copies(ins, scr):
        _, inner, outer = on_line(count)
        to = outer if hop >= mid else inner
        return [push(ins[i], scr[2 + i], scr[0], i, to) for i in range(total)]

    def start(ins, outs, scr):
        depth, _, _ = on_line(count)

        @pl.when(depth == sender)
        def _():
            for copy in copies(ins, scr):
                copy.start()

    def finish(ins, outs, scr):
        depth, _, _ = on_line(count)
        sent = copies(ins, scr)
        loads = [pltpu.make_async_copy(ins[i], scr[2 + total + i], scr[1].at[0, i]) for i in range(total)]
        stores = [pltpu.make_async_copy(scr[2 + total + i], outs[i], scr[1].at[1, i]) for i in range(total)]
        for load in loads:
            load.start()

        @pl.when(depth == sender)
        def _():
            for copy in sent:
                copy.wait_send()

        for load in loads:
            load.wait()

        @pl.when(depth == taker)
        def _():
            for i in range(total):
                sent[i].wait_recv()
                came, own = scr[2 + i], scr[2 + total + i]
                if hop >= mid:
                    own[...] = came[...]
                else:
                    own[...] = (own[...].astype(F32) + came[...].astype(F32)).astype(BF)

        for store in stores:
            store.start()
        for store in stores:
            store.wait()

    buffers = [pltpu.VMEM(array.shape, BF) for array in arrays]
    return Task(
        [(array, ANY) for array in arrays],
        [(struct(array.shape, BF), ANY) for array in arrays],
        [pltpu.SemaphoreType.DMA((2, total)), pltpu.SemaphoreType.DMA((2, total))] + buffers * 2,
        start,
        finish,
        ("inner", "outer"),
    )


def line_kernel(count, nch, items, ins, outs, scratch):
    mid = count // 2
    hops = 2 * mid - 1
    s1, r1, s2, r2, s3, r3, s4, r4, sx, core_sem, from_core = scratch[:11]
    free = list(scratch[11:])
    in1, res = [], []
    for (kind, k, done, _), mine, out in zip(items, ins, outs):
        in1.append(free.pop(0) if needs_in(kind, done, mid) else None)
        if done >= hops:
            res.append(mine)
        else:
            res.append(free.pop(0) if needs_res(kind, k) else out)
    depth, inner, outer = on_line(count)
    peers = [chip_peer(k) for k in range(nch)]
    barrier = pltpu.get_barrier_semaphore()

    def tell(device):
        pl.semaphore_signal(barrier, inc=1, device_id=device, device_id_type=pl.DeviceIdType.MESH)

    tell(inner)
    tell(core_peer())
    for k in range(1, nch):
        tell(peers[k])

    @pl.when(depth > 0)
    def _():
        tell(outer)
        pl.semaphore_wait(barrier, nch + 2)

    @pl.when(depth == 0)
    def _():
        pl.semaphore_wait(barrier, nch + 1)

    chunks = []
    for i, (kind, _, _, _) in enumerate(items):
        tall = ins[i].shape[0]
        cut = tall // 32 * 16
        chunks += [(i, 0, cut), (i, cut, tall - cut)] if kind == "block" else [(i, 0, tall)]

    def view(refs, c):
        i, lo, size = chunks[c]
        return refs[i].at[pl.ds(lo, size), :]

    def copy(src, dst, send, recv, i, device):
        return pltpu.make_async_remote_copy(
            src_ref=src,
            dst_ref=dst,
            send_sem=send.at[i],
            recv_sem=recv.at[i],
            device_id=device,
            device_id_type=pl.DeviceIdType.MESH,
        )

    def facts(c, place):
        kind, k, done, _ = items[chunks[c][0]]
        middle = place == mid - 1
        return dict(
            kind=kind,
            k=k,
            over=done >= hops,
            takes=place > 0 and place - 1 >= done,
            gives=place >= done,
            trade=middle and mid - 1 >= done,
            known=2 * mid - 2 - place < done,
            outward=place > 0 and 2 * mid - 1 - place >= done,
        )

    def sent_from(c, fact):
        return in1 if fact["takes"] or fact["kind"] == "small" else ins

    def hop1(c, fact):
        return copy(view(sent_from(c, fact), c), view(in1, c), s1, r1, c, inner)

    def hop2(c, fact):
        return copy(view(sent_from(c, fact), c), view(res, c), s2, r2, c, inner)

    def came(c, send, recv):
        return copy(view(res, c), view(res, c), send, recv, c, outer)

    def hop4(c, fact):
        i = chunks[c][0]
        if fact["kind"] == "block" and fact["k"]:
            return [copy(view(res, c), view(outs, c), s4, r4, c, peers[fact["k"]])]
        if fact["kind"] == "small":
            return [push(res[i], outs[i].at[j], sx, j, peers[j]) for j in range(1, nch)]
        return []

    small = next(i for i, item in enumerate(items) if item[0] == "small")
    to_core = push(ins[small], from_core, core_sem, 0, core_peer())
    to_core.start()

    def inward(c, fact):
        i = chunks[c][0]
        if fact["over"] or fact["known"]:
            return None
        if fact["kind"] == "small":
            to_core.wait()
            value = ins[i][...] + from_core[...]
            if fact["takes"]:
                hop1(c, fact).wait_recv()
                value = value + in1[i][...]
            in1[i][...] = value
        elif fact["takes"]:
            hop1(c, fact).wait_recv()
            value = view(ins, c)[...].astype(F32) + view(in1, c)[...].astype(F32)
            view(in1, c)[...] = value.astype(BF)
        if fact["trade"]:
            out = hop2(c, fact)
        elif fact["gives"]:
            out = hop1(c, fact)
        else:
            return None
        out.start()
        return out

    def outward(c, fact):
        i = chunks[c][0]
        if not fact["over"]:
            if fact["trade"]:
                hop2(c, fact).wait_recv()
                value = view(sent_from(c, fact), c)[...].astype(F32) + view(res, c)[...].astype(F32)
                view(res, c)[...] = value.astype(ins[i].dtype)
            elif fact["known"]:
                view(res, c)[...] = view(ins, c)[...]
            else:
                came(c, s3, r3).wait_recv()
            if fact["outward"]:
                came(c, s3, r3).start()
        if fact["kind"] == "small":
            outs[i][0] = res[i][...]
        elif fact["over"] and not hop4(c, fact):
            view(outs, c)[...] = view(ins, c)[...]
        for item in hop4(c, fact):
            item.start()

    total = len(chunks)
    for place in range(mid):

        @pl.when(depth == place)
        def _(place=place):
            lag = 2 + 3 * (mid - 1 - place)
            all_facts = [facts(c, place) for c in range(total)]
            flying = []
            for i in range(total + lag):
                if i < total:
                    if len(flying) >= 2:
                        flying.pop(0).wait_send()
                    started = inward(i, all_facts[i])
                    if started is not None:
                        flying.append(started)
                if i >= lag:
                    outward(i - lag, all_facts[i - lag])
            for item in flying:
                item.wait_send()
            for c, fact in enumerate(all_facts):
                if fact["outward"] and not fact["over"]:
                    came(c, s3, r3).wait_send()
                for item in hop4(c, fact):
                    item.wait()


def needs_in(kind, done, mid):
    return kind == "small" or done < mid - 1


def needs_res(kind, k):
    return kind == "small" or (kind == "block" and k > 0)


def line_sum(cid, nch, items):
    count = lax.axis_size("rep")
    mid = count // 2
    arrays = [item[3] for item in items]
    scratch = []
    for kind, k, done, array in items:
        if needs_in(kind, done, mid):
            scratch.append(pltpu.VMEM(array.shape, array.dtype))
        if done < 2 * mid - 1 and needs_res(kind, k):
            scratch.append(pltpu.VMEM(array.shape, array.dtype))
    total = 2 * len(items)
    small = next(array for kind, _, _, array in items if kind == "small")
    fixed = [pltpu.SemaphoreType.DMA((total,))] * 8
    fixed += [pltpu.SemaphoreType.DMA((2, nch)), pltpu.SemaphoreType.DMA((2, 1)), pltpu.VMEM(small.shape, F32)]
    vmem = pl.BlockSpec(memory_space=pltpu.VMEM)
    shapes = [
        struct(((nch,) if kind == "small" else ()) + array.shape, array.dtype) for kind, _, _, array in items
    ]

    def kernel(*refs):
        refs = list(refs)
        line_kernel(count, nch, items, refs[: len(items)], refs[len(items) : 2 * len(items)], refs[2 * len(items) :])

    return pl.pallas_call(
        kernel,
        in_specs=[vmem] * len(items),
        out_specs=[vmem] * len(items),
        out_shape=shapes,
        scratch_shapes=fixed + scratch,
        compiler_params=pltpu.CompilerParams(collective_id=cid, has_side_effects=True, vmem_limit_bytes=63 << 20),
        cost_estimate=pl.CostEstimate(flops=0, bytes_accessed=400 << 20, transcendentals=0),
        name="line_sum",
    )(*arrays)


def unpack_kernel(nch, inner, index, *refs):
    out = refs[-1]
    local = inner // nch
    step = local // HEADDIM
    for layer in range(LAYERS):

        @pl.when(pl.program_id(0) == layer)
        def _():
            blocks = refs[layer * nch : (layer + 1) * nch]
            bc = 0.0
            for k in range(nch):
                of = jnp.bitwise_xor(index[0], k)
                for j in range(2):
                    to = pl.multiple_of(of * local + j * inner, local)
                    out[0, pl.ds(to, local), :] = blocks[k][j * local : (j + 1) * local, :].astype(F32)
                bc = bc + blocks[k][2 * local : 2 * local + 2 * STATE, :].astype(F32)
                to = pl.multiple_of(of * step + 2 * inner + 2 * STATE, step)
                at = 2 * local + 2 * STATE
                out[0, pl.ds(to, step), :] = blocks[k][at : at + STEPS, :].astype(F32)[:step]
            out[0, 2 * inner : 2 * inner + 2 * STATE, :] = bc


def unpack(index, blocks, inner, columns):
    nch = len(blocks[0])
    tall, part = blocks[0][0].shape
    specs = [pl.BlockSpec((tall, part), lambda i, idx: (0, 0))] * nch
    return pl.pallas_call(
        functools.partial(unpack_kernel, nch, inner),
        grid_spec=pltpu.PrefetchScalarGridSpec(
            num_scalar_prefetch=1,
            grid=(LAYERS,),
            in_specs=specs * LAYERS,
            out_specs=pl.BlockSpec((1, columns, part), lambda i, idx: (i, 0, 0)),
        ),
        out_shape=struct((LAYERS, columns, part), F32),
        compiler_params=pltpu.CompilerParams(vmem_limit_bytes=60 << 20),
        name="unpack",
    )(index, *sum(blocks, []))


def body(
    tokens,
    lengths,
    order,
    norm_gain,
    in_proj,
    conv_weight,
    conv_bias,
    dt_bias,
    a_log,
    skip,
    gate_norm,
    out_proj,
    cotangent,
):
    n = lax.axis_size("shard")
    nch = n // 2
    me = lax.axis_index("shard")
    chip, core = me // 2, me % 2
    index = jnp.stack([chip, core]).astype(jnp.int32)
    base = lax.axis_index("rep") * n
    width = tokens.shape[2]
    inner = gate_norm.shape[1] * n
    channels = conv_bias.shape[1] * n
    local = inner // nch
    ng = local // GROUP
    rows = nch * HALF
    sizes = (norm_gain.shape[1], gate_norm.shape[1], conv_bias.shape[1], dt_bias.shape[1])
    transposed = jnp.swapaxes(in_proj, 1, 2)

    def tiled(x):
        return jnp.pad(x, ((0, 0), (0, 128 - x.shape[1])))

    def wide(x):
        return jnp.pad(x, ((0, 0),) * (x.ndim - 1) + ((0, width - x.shape[-1]),))

    top = wide(jnp.concatenate([norm_gain, gate_norm, tiled(dt_bias), tiled(a_log), tiled(skip)], 1))
    small = jnp.concatenate([top[:, None], wide(conv_weight), wide(conv_bias)[:, None]], 1)
    small = jnp.pad(small, ((0, 0), (0, 2), (0, 0))).reshape(8 * LAYERS, width)

    seqs = base + 2 * jnp.bitwise_xor(chip, jnp.arange(nch)) + core
    listing = jnp.arange(order.shape[0])
    slots = jnp.sum(jnp.where(order[None] == seqs[:, None], listing[None], 0), axis=1) - base
    slots = (jnp.bitwise_xor(core, slots % 2) * nch + jnp.bitwise_xor(chip, slots // 2)).astype(jnp.int32)
    valid = lengths[base + me]
    halves = (0, 1)
    mask = [
        jnp.broadcast_to(((jnp.arange(HALF) + h * HALF) < valid).astype(F32)[:, None], (HALF, 128)) for h in halves
    ]
    gout = [
        jnp.where(mask[h][:, 0:1] > 0, cotangent[0, h * HALF : (h + 1) * HALF], jnp.zeros((), BF)) for h in halves
    ]

    w0, toks, smalls, wo0, wo1 = start_up(transposed, tokens, small, out_proj, nch, inner, channels)
    gains, pm, pbc = make_params(index, smalls, nch, ng, sizes)
    xs, stream0 = pick(slots, toks, gains, nch)
    weights = [weight_ins(w0, wo0, pm, pbc, 0), None]

    def picked(h):
        return [(xs, pl.BlockSpec((None, None, HALF, width), lambda g, k=k: (h, k, 0, 0))) for k in range(nch)]

    def others(array, lanes=None, lane_block=0):
        return [row_of(array, k, lanes, lane_block) for k in range(nch - 1)]

    stream0 = [row_of(stream0, h) for h in halves]
    gain = [row_of(gains, layer) for layer in range(LAYERS)]
    flow1 = [(cotangent, pl.BlockSpec((None, HALF, width), lambda g, h=h: (0, h, 0))) for h in halves]

    r00, ((fetched,),) = run_fwd(
        2, picked(0), weights[0], None, [fetch_task(transposed, 1, nch, inner, channels)]
    )
    r01, ((branch00, stream10, norm10, scale00),) = run_fwd(
        3, picked(1), weights[0], r00, [owner_fwd(r00["parts"], stream0[0], mask[0], gain[1], None, inner)]
    )
    _, (near10,), (branch01, stream11, norm11, scale01), (w1,) = launch(
        "between_layers",
        4,
        1,
        None,
        [],
        [],
        [],
        [
            gather_task([norm10], nch),
            owner_fwd(r01["parts"], stream0[1], mask[1], gain[1], None, inner),
            finish_task(transposed, fetched, 1, nch, inner, channels),
        ],
    )
    weights[1] = weight_ins(w1, wo1, pm, pbc, 1)
    r10, ((near11,),) = run_fwd(5, [full(norm10)] + others(near10), weights[1], None, [gather_task([norm11], nch)])
    r11, ((branch10, out0, scal10),) = run_fwd(
        6,
        [full(norm11)] + others(near11),
        weights[1],
        r10,
        [owner_fwd(r10["parts"], full(stream10), mask[0], None, full(gout[0]), inner)],
    )
    _, (cot1, near_s0), (branch11, out1, scal11, near_s1) = launch(
        "turn",
        7,
        1,
        None,
        [],
        [],
        [],
        [
            gather_task([gout[1], scal10], nch),
            owner_fwd(r11["parts"], full(stream11), mask[1], None, full(gout[1]), inner, True),
        ],
    )
    output = jnp.concatenate([out0, out1], 0)[None]

    b11, ((cot0,),) = run_bwd(
        8,
        [full(gout[1])] + others(cot1),
        [full(scal11)] + others(near_s1),
        weights[1],
        r11,
        r10,
        None,
        [gather_task([gout[0]], nch)],
    )
    b10, ((gg11, flow11, gb01),) = run_bwd(
        9,
        [full(gout[0])] + others(cot0),
        [full(scal10)] + others(near_s0),
        weights[1],
        r10,
        None,
        b11,
        [owner_bwd(b11["parts"], full(stream11), gain[1], flow1[1], mask[1], branch01, scale01, inner)],
    )

    def flat(x):
        return x.reshape(rows, -1)

    def grads(first, second, back_a, back_b):
        pieces = [first["xall"], second["xall"]]
        for name in ("gpz", "gpx", "gpbc", "gnorm", "gall"):
            pieces += [flat(back_a[name]), flat(back_b[name])]
        return grads_task(nch, *pieces)

    _, (near_b1,), (gg10, flow10, gb00), last_grads = launch(
        "grads_last",
        10,
        1,
        None,
        [],
        [],
        [],
        [
            gather_task([gb01], nch),
            owner_bwd(b10["parts"], full(stream10), gain[1], flow1[0], mask[0], branch00, scale00, inner),
            grads(r10, r11, b10, b11),
        ],
    )
    in1, rows1 = list(last_grads[:nch]), list(last_grads[nch:])
    hops = 2 * (lax.axis_size("rep") // 2) - 1
    batches = [[in1[nch - 1 - i], rows1[i]] for i in range(3)]
    passed = [0, 0, 0]

    def hop_tasks(step):
        return [hop_task(passed[i], batches[i]) for i in range(step + 1) if passed[i] < hops]

    def hopped(step, results):
        results = list(results)
        for i in range(step + 1):
            if passed[i] < hops:
                batches[i] = list(results.pop(0))
                passed[i] += 1

    def payload(own, near):
        tile = width // 128
        gs = [(own, pl.BlockSpec((HALF, width), lambda g: (0, 0)))] + others(near, width)
        ts = [(own, pl.BlockSpec((HALF, 128), lambda g: (0, tile)))] + others(near, 128, tile)
        return gs, ts

    b01, ((near_b0,), *more) = run_bwd(
        11, *payload(gb01, near_b1), weights[0], r01, r00, None, [gather_task([gb00], nch)] + hop_tasks(0)
    )
    hopped(0, more)
    b00, ((gg01, gtok1), *more) = run_bwd(
        12,
        *payload(gb00, near_b0),
        weights[0],
        r00,
        None,
        b01,
        [owner_bwd(b01["parts"], stream0[1], gain[0], full(flow11), None, None, None, inner)] + hop_tasks(1),
    )
    hopped(1, more)
    _, (gg00, gtok0), first_grads, *more = launch(
        "grads_first",
        13,
        1,
        None,
        [],
        [],
        [],
        [
            owner_bwd(b00["parts"], stream0[0], gain[0], full(flow10), None, None, None, inner),
            grads(r00, r01, b00, b01),
        ]
        + hop_tasks(2),
    )
    hopped(2, more)
    in0, rows0 = list(first_grads[:nch]), list(first_grads[nch:])
    grad_tokens = jnp.concatenate([gtok0, gtok1], 0)[None]

    def packed(a, b, ga, gb):
        bc = a["sgbc"] + b["sgbc"]
        tail = jnp.pad(bc[:, 2 * STATE :], ((0, 0), (0, GROUP - STATE)))
        return [(a["sgm"] + b["sgm"]).reshape(8 * ng, GROUP), bc[:, : 2 * STATE], tail, (ga + gb)[0].reshape(-1, GROUP)]

    vectors = jnp.concatenate(packed(b00, b01, gg00, gg01) + packed(b10, b11, gg10, gg11), 0)
    for i in range(3):
        in1[nch - 1 - i], rows1[i] = batches[i]
    items = []
    for i in range(3):
        items += [("block", nch - 1 - i, passed[i], in1[nch - 1 - i]), ("rows", 0, passed[i], rows1[i])]
    items += [("block", k, 0, in1[k]) for k in range(nch - 4, -1, -1)] + [("rows", 0, 0, rows1[3])]
    items += [("block", k, 0, in0[k]) for k in range(nch - 1, 0, -1)] + [("small", 0, 0, vectors)]
    items += [("block", 0, 0, in0[0])] + [("rows", 0, 0, item) for item in rows0]
    summed = line_sum(14, nch, items)
    sums = summed[items.index(next(item for item in items if item[0] == "small"))]

    def result(array):
        return next(out for item, out in zip(items, summed) if item[3] is array)

    in0, in1 = [result(item) for item in in0], [result(item) for item in in1]
    rows0 = jnp.concatenate([result(item) for item in rows0], 0)
    rows1 = jnp.concatenate([result(item) for item in rows1], 0)
    grads_in = jnp.swapaxes(unpack(index, [in0, in1], inner, in_proj.shape[2]), 1, 2)
    grads_out = jnp.stack([rows0, rows1]).astype(F32)

    sums = jnp.stack([lax.dynamic_index_in_dim(sums, jnp.bitwise_xor(chip, q), 0, keepdims=False) for q in range(nch)])
    sums = sums.reshape(nch, LAYERS, -1, GROUP)
    main = sums[:, :, : 8 * ng].reshape(nch, LAYERS, ng, 8, GROUP).transpose(1, 3, 0, 2, 4)
    main = main.reshape(LAYERS, 8, inner)
    bc = sums[:, :, 8 * ng : 8 * ng + 8].sum(0)
    steps = sums[:, :, 8 * ng + 8 : 8 * ng + 16, : local // HEADDIM].transpose(1, 2, 0, 3).reshape(LAYERS, 8, -1)
    grad_gain = sums[:, :, 8 * ng + 16 :].sum(0).reshape(LAYERS, width)
    conv = jnp.concatenate([main[:, :5], bc[:, :5]], 2)
    skips = main[:, 5].reshape(LAYERS, -1, HEADDIM).sum(-1)

    def own(x):
        part = x.shape[-1] // n
        return lax.dynamic_slice_in_dim(x, me * part, part, x.ndim - 1)

    conv = own(conv)
    return (
        output,
        grad_tokens,
        own(grad_gain),
        grads_in,
        conv[:, :4],
        conv[:, 4],
        own(steps[:, 4]),
        own(steps[:, 5]),
        own(skips),
        own(main[:, 6]),
        grads_out,
    )


def solution(mesh):
    in_specs = (
        P(("rep", "shard"), None, None),
        P(),
        P(),
        P(None, "shard"),
        P(None, "shard", None),
        P(None, None, "shard"),
        P(None, "shard"),
        P(None, "shard"),
        P(None, "shard"),
        P(None, "shard"),
        P(None, "shard"),
        P(None, "shard", None),
        P(("rep", "shard"), None, None),
    )
    out_specs = (
        P(("rep", "shard"), None, None),
        P(("rep", "shard"), None, None),
        P(None, "shard"),
        P(None, "shard", None),
        P(None, None, "shard"),
        P(None, "shard"),
        P(None, "shard"),
        P(None, "shard"),
        P(None, "shard"),
        P(None, "shard"),
        P(None, "shard", None),
    )
    return jax.shard_map(body, mesh=mesh, in_specs=in_specs, out_specs=out_specs, check_vma=False)
```
